32 devices in a mesh: mp: 8 (over z, x), dp: 4 (over y, core).
Axes of the slice: x: 2, y: 2, z: 4, core: 2. Of those that a mesh axis runs over, the one named last changes fastest.
Arguments:
- pre_act: bfloat16 [512, 36864], P('dp', 'mp'), may hold values from -5 to 5
- cotangent: bfloat16 [512, 10240], P('mp', 'dp'), may hold values from -6 to 6
- down_weight: bfloat16 [36864, 10240], P('mp', 'dp'), may hold values from -0.03125 to 0.03125
- first_moment: bfloat16 [36864, 10240], P('mp', 'dp'), may hold values from -4.0625 to 4.0625
- second_moment: bfloat16 [36864, 10240], P('mp', 'dp'), may hold values from 1.0234375 to 51
Outputs:
- input_grad: bfloat16 [512, 36864], P('dp', 'mp')
- step_update: bfloat16 [36864, 10240], P('mp', 'dp')
The draws below stay inside these ranges and needn't reach their ends.
All inputs are finite; a program needn't handle non-finite values.
Results may differ from the reference program's by a relative error of at most 0.023.
Values may be sent and summed in bfloat16 or wider, within the bound.
A program may use at most 192 MiB of HBM per device.

```python
import math
import jax
import jax.numpy as jnp
from jax import lax

D = 10240
FF = 36864
STEP = 20
TOKENS = 512
N_MP = 8
N_DP = 4


def levels(stream_key, shape, pieces, low, high):
    gain, own = 1.0, jax.random.fold_in(stream_key, 6)
    for dim, blocks in pieces:
        steps = jnp.exp(jax.random.uniform(jax.random.fold_in(own, dim), (blocks,), jnp.float32, low / len(pieces), high / len(pieces)))
        gain = gain * jnp.repeat(steps, shape[dim] // blocks).reshape([-1 if axis == dim else 1 for axis in range(len(shape))])
    return gain


def gaussian(rng, shape, spread, limit, split=(), kind=jnp.bfloat16):
    array = spread * jax.random.normal(rng, shape, jnp.float32)
    if split:
        array = array * levels(rng, shape, split, -0.22, 0.18)
    return jnp.clip(array, -limit, limit).astype(kind)


def setup_inputs(seed: int = 0) -> dict:
    streams_of = jax.random.split(jax.random.key(seed), 6)
    pre_act = gaussian(streams_of[0], (TOKENS, FF), 1.0, 5.0, ((0, 4), (1, 8)))
    cotangent = gaussian(streams_of[1], (TOKENS, D), 1.0, 6.0, ((0, 8), (1, 4)))
    down_weight = gaussian(streams_of[2], (FF, D), FF ** -0.5, 0.03125, ((0, 8), (1, 4)))
    first_moment = gaussian(streams_of[3], (FF, D), (0.03 * TOKENS ** 0.5), 4.0625, ((0, 8), (1, 4)))
    second_moment = jnp.clip(jnp.exp(math.log(51.0) - 3.9086586 * jax.random.uniform(streams_of[4], (FF, D), jnp.float32) ** levels(streams_of[4], (FF, D), ((0, 8), (1, 4)), -0.2, 0.2)), 1.0234375, 51.0).astype(jnp.bfloat16)
    return dict(pre_act=pre_act, cotangent=cotangent, down_weight=down_weight, first_moment=first_moment, second_moment=second_moment)


gelu_scale = 0.7978845608028654
gelu_cubic = 0.044715
beta_one = 0.9
beta_two = 0.95
epsilon = 1e-08

def gelu_parts(values):
    tangent = jnp.tanh(gelu_scale * (values + gelu_cubic * values * values * values))
    output = 0.5 * values * (1.0 + tangent)
    slopes = 0.5 * (1.0 + tangent) + 0.5 * values * (1.0 - tangent * tangent) * gelu_scale * (1.0 + 3.0 * gelu_cubic * values * values)
    return (output, slopes)

def adam_update(gradient, first_moment, second_moment):
    moment_one = beta_one * first_moment.astype(jnp.float32) + (1.0 - beta_one) * gradient
    moment_two = beta_two * second_moment.astype(jnp.float32) + (1.0 - beta_two) * gradient * gradient
    corrected = moment_one / (1.0 - beta_one ** STEP)
    scaled = jnp.sqrt(moment_two / (1.0 - beta_two ** STEP))
    return (corrected / (scaled + epsilon)).astype(jnp.bfloat16)

def reference(pre_act, cotangent, down_weight, first_moment, second_moment):
    output, slopes = gelu_parts(pre_act.astype(jnp.float32))
    hidden = output.astype(jnp.bfloat16)
    columns = D // N_DP

    def add_block(block_index, summed):
        offset = (block_index * columns).astype(jnp.int32)
        cot_block = lax.dynamic_slice_in_dim(cotangent, offset, columns, 1)
        weight_block = lax.dynamic_slice_in_dim(down_weight, offset, columns, 1)
        partial_sum = lax.dot_general(cot_block, weight_block, (((1,), (1,)), ((), ())), preferred_element_type=jnp.float32)
        rounded = lax.optimization_barrier(partial_sum.astype(jnp.bfloat16))
        return summed + rounded.astype(jnp.float32)
    hidden_grad = lax.fori_loop(0, N_DP, add_block, jnp.zeros((TOKENS, FF), jnp.float32))
    input_grad = (hidden_grad * slopes).astype(jnp.bfloat16)
    unit_rows = FF // N_MP

    def block_update(block_index):
        offset = (block_index * unit_rows).astype(jnp.int32)
        hidden_block = lax.dynamic_slice_in_dim(hidden, offset, unit_rows, 1)
        gradient = lax.dot_general(hidden_block, cotangent, (((0,), (0,)), ((), ())), preferred_element_type=jnp.float32)
        moment_block = lax.dynamic_slice_in_dim(first_moment, offset, unit_rows, 0)
        second_block = lax.dynamic_slice_in_dim(second_moment, offset, unit_rows, 0)
        return adam_update(gradient, moment_block, second_block)
    stacked = lax.map(block_update, jnp.arange(N_MP, dtype=jnp.int32))
    return (input_grad, stacked.reshape(FF, D))
```

```python
import functools

import jax
import jax.numpy as jnp
from jax import lax
from jax.experimental import pallas as pl
from jax.experimental.pallas import tpu as pltpu
from jax.sharding import PartitionSpec as P

STEP = 20

MESH = pl.DeviceIdType.MESH

gelu_scale = 0.7978845608028654
gelu_cubic = 0.044715
beta_one = 0.9
beta_two = 0.95
epsilon = 1e-08


def gelu_output(values):
    tangent = jnp.tanh(gelu_scale * (values + gelu_cubic * values * values * values))
    return 0.5 * values * (1.0 + tangent)


def gelu_slopes(values):
    tangent = jnp.tanh(gelu_scale * (values + gelu_cubic * values * values * values))
    return 0.5 * (1.0 + tangent) + 0.5 * values * (1.0 - tangent * tangent) * gelu_scale * (
        1.0 + 3.0 * gelu_cubic * values * values
    )


def adam_step(gradient, first, second):
    gain = (1.0 - beta_one) / (1.0 - beta_one**STEP)
    spread = 1.0 / ((1.0 - beta_two**STEP) * gain * gain)
    moment_one = (beta_one / (1.0 - beta_one)) * first + gradient
    moment_two = (beta_two * spread) * second + ((1.0 - beta_two) * spread) * (gradient * gradient)
    scaled = moment_two * lax.rsqrt(moment_two)
    return moment_one * pl.reciprocal(scaled + epsilon / gain, approx=True)


def exchange_kernel(
    chunks, pieces, block,
    pre_ref, cot_ref, weight_ref,
    cot_all, hid_all, mine_ref, away_ref,
    weight, hidden, total, part, other,
    weight_sem, own_sem, ring_send, ring_recv, hid_send, hid_recv, fwd_send, fwd_recv,
    pair_send, pair_recv,
):
    mp, dp = lax.axis_index("mp"), lax.axis_index("dp")
    tokens, features = cot_ref.shape
    units = weight_ref.shape[0]
    wide = features // chunks
    tall = units // pieces
    rows = pre_ref.shape[0]

    x, z = mp % 2, mp // 2
    place = z + x * (7 - 2 * z)

    def index_of(position):
        p = (position + 16) % 8
        side = p // 4
        return 2 * (p + side * (7 - 2 * p)) + side

    ring = (index_of(place + 1), index_of(place - 1))
    core, y = dp % 2, dp // 2
    sibling = 2 * y + (1 - core)
    across = 2 * (1 - y) + core

    def columns(k):
        return pl.ds(k * wide, wide)

    loads = []
    for k in range(chunks):
        load = pltpu.make_async_copy(
            weight_ref.at[:, columns(k)], weight.at[:, columns(k)], weight_sem.at[k]
        )
        load.start()
        loads.append(load)

    barrier = pltpu.get_barrier_semaphore()
    for position in ring:
        pl.semaphore_signal(barrier, inc=1, device_id={"mp": position}, device_id_type=MESH)
    for position in (sibling, across):
        pl.semaphore_signal(barrier, inc=1, device_id={"dp": position}, device_id_type=MESH)
    cot_all[mp] = cot_ref[...]
    pl.semaphore_wait(barrier, 4)

    def hops(k, way):
        return 4 if k % 2 == way else 3

    def ring_copy(k, hop, way):
        origin = index_of(place - hop if way == 0 else place + hop)
        return pltpu.make_async_remote_copy(
            src_ref=cot_all.at[origin, :, columns(k)],
            dst_ref=cot_all.at[origin, :, columns(k)],
            send_sem=ring_send.at[k, hop, way],
            recv_sem=ring_recv.at[k, hop, way],
            device_id={"mp": ring[way]},
            device_id_type=MESH,
        )

    def ring_wait(k, hop, way):
        origin = index_of(place - hop - 1 if way == 0 else place + hop + 1)
        pltpu.make_async_remote_copy(
            src_ref=cot_all.at[origin, :, columns(k)],
            dst_ref=cot_all.at[origin, :, columns(k)],
            send_sem=ring_send.at[k, hop, way],
            recv_sem=ring_recv.at[k, hop, way],
            device_id={"mp": ring[way]},
            device_id_type=MESH,
        ).wait_recv()

    def hid_rows(j):
        return pl.ds(j * tall, tall)

    def hid_copy(j, which):
        return pltpu.make_async_remote_copy(
            src_ref=hidden.at[hid_rows(j), :],
            dst_ref=hid_all.at[dp, hid_rows(j), :],
            send_sem=hid_send.at[j, which],
            recv_sem=hid_recv.at[j, which],
            device_id={"dp": (across, sibling)[which]},
            device_id_type=MESH,
        )

    def hid_wait(j, which):
        origin = (across, sibling)[which]
        pltpu.make_async_remote_copy(
            src_ref=hidden.at[hid_rows(j), :],
            dst_ref=hid_all.at[origin, hid_rows(j), :],
            send_sem=hid_send.at[j, which],
            recv_sem=hid_recv.at[j, which],
            device_id={"dp": origin},
            device_id_type=MESH,
        ).wait_recv()

    def forward_copy(j, origin):
        return pltpu.make_async_remote_copy(
            src_ref=hid_all.at[origin, hid_rows(j), :],
            dst_ref=hid_all.at[origin, hid_rows(j), :],
            send_sem=fwd_send.at[j],
            recv_sem=fwd_recv.at[j],
            device_id={"dp": sibling},
            device_id_type=MESH,
        )

    sent = []
    kept = []
    for k in range(chunks):
        for way in (0, 1):
            copy = ring_copy(k, 0, way)
            copy.start()
            sent.append(copy)

    for j in range(pieces):
        values = pre_ref[:, j * tall : (j + 1) * tall].astype(jnp.float32)
        hidden[hid_rows(j), :] = gelu_output(values).T.astype(jnp.bfloat16)
        for which in (0, 1):
            copy = hid_copy(j, which)
            copy.start()
            sent.append(copy)
        copy = pltpu.make_async_copy(
            hidden.at[hid_rows(j), :], hid_all.at[dp, hid_rows(j), :], own_sem.at[j]
        )
        copy.start()
        kept.append(copy)

    def multiply(k, first, last):
        loads[k].wait()
        cot = cot_all[:, :, k * wide : (k + 1) * wide].reshape(8 * tokens, wide)

        def one(i, carry):
            at = pl.ds(pl.multiple_of(i * block, block), block)
            product = lax.dot_general(
                cot,
                weight[at, columns(k)],
                (((1,), (1,)), ((), ())),
                preferred_element_type=jnp.float32,
            )
            if not first:
                product = product + total[:, at]
            if not last:
                total[:, at] = product
                return carry
            part[:, :, at] = product.astype(jnp.bfloat16).reshape(4, rows, block)
            for side in (0, 1):
                pair_copy(i, side).start()
            return carry

        lax.fori_loop(0, units // block, one, 0)

    def pair_copy(i, side):
        at = pl.ds(pl.multiple_of(i * block, block), block)
        return pltpu.make_async_remote_copy(
            src_ref=part.at[2 * side + 1 - core, :, at],
            dst_ref=other.at[side, :, at],
            send_sem=pair_send.at[i, side],
            recv_sem=pair_recv.at[i, side],
            device_id={"dp": sibling},
            device_id_type=MESH,
        )

    for step in range(chunks + 3):
        done = None
        for k in range(chunks):
            hop = step - k
            if hop < 0 or hop > 3:
                continue
            for way in (0, 1):
                if hop < hops(k, way):
                    ring_wait(k, hop, way)
                    if hop + 1 < hops(k, way):
                        copy = ring_copy(k, hop + 1, way)
                        copy.start()
                        sent.append(copy)
            if hop == 3:
                done = k
        if 0 <= step - 2 < pieces:
            hid_wait(step - 2, 0)
            copy = forward_copy(step - 2, across)
            copy.start()
            sent.append(copy)
        if done is not None:
            multiply(done, done == 0, done == chunks - 1)

    def combine(i, carry):
        at = pl.ds(pl.multiple_of(i * block, block), block)
        for side in (0, 1):
            pair_copy(i, side).wait()
        mine = part[2 * y + core, :, at].astype(jnp.float32) + other[y, :, at].astype(jnp.float32)
        away = part[2 * (1 - y) + core, :, at].astype(jnp.float32) + other[1 - y, :, at].astype(
            jnp.float32
        )
        mine_ref[:, at] = mine.astype(jnp.bfloat16)
        away_ref[:, at] = away.astype(jnp.bfloat16)
        return carry

    lax.fori_loop(0, units // block, combine, 0)

    for j in range(pieces):
        hid_wait(j, 1)
        forward_copy(j, 2 * (1 - y) + (1 - core)).wait_recv()
    for copy in sent:
        copy.wait_send()
    for copy in kept:
        copy.wait()


def exchange(pre_act, cotangent, weight):
    rows, units = pre_act.shape
    tokens, features = cotangent.shape
    chunks, pieces, block = 5, 6, 512
    vmem = pl.BlockSpec(memory_space=pltpu.VMEM)
    hbm = pl.BlockSpec(memory_space=pl.ANY)
    bf16 = jnp.bfloat16
    dma = pltpu.SemaphoreType.DMA
    return pl.pallas_call(
        functools.partial(exchange_kernel, chunks, pieces, block),
        out_shape=(
            jax.ShapeDtypeStruct((8, tokens, features), bf16),
            jax.ShapeDtypeStruct((4, units, rows), bf16),
            jax.ShapeDtypeStruct((rows, units), bf16),
            jax.ShapeDtypeStruct((rows, units), bf16),
        ),
        in_specs=[vmem, vmem, hbm],
        out_specs=(vmem, hbm, vmem, vmem),
        scratch_shapes=[
            pltpu.VMEM((units, features), bf16),
            pltpu.VMEM((units, rows), bf16),
            pltpu.VMEM((8 * tokens, units), jnp.float32),
            pltpu.VMEM((4, rows, units), bf16),
            pltpu.VMEM((2, rows, units), bf16),
            dma((chunks,)),
            dma((pieces,)),
            dma((chunks, 4, 2)),
            dma((chunks, 4, 2)),
            dma((pieces, 2)),
            dma((pieces, 2)),
            dma((pieces,)),
            dma((pieces,)),
            dma((units // block, 2)),
            dma((units // block, 2)),
        ],
        compiler_params=pltpu.CompilerParams(
            collective_id=0, has_side_effects=True, vmem_limit_bytes=60 * 2**20
        ),
        name="exchange",
    )(pre_act, cotangent, weight)


def update_kernel(tile, hid_ref, cot_ref, first_ref, second_ref, out_ref):
    hidden = jnp.concatenate([hid_ref[i] for i in range(hid_ref.shape[0])], axis=1)
    for start in range(0, out_ref.shape[1], tile):
        at = slice(start, start + tile)
        gradient = jnp.dot(hidden, cot_ref[:, at], preferred_element_type=jnp.float32)
        out_ref[:, at] = adam_step(
            gradient, first_ref[:, at].astype(jnp.float32), second_ref[:, at].astype(jnp.float32)
        ).astype(jnp.bfloat16)


def update(hid_all, cot_whole, first_moment, second_moment):
    units, features = first_moment.shape
    groups, _, rows = hid_all.shape
    tall = 256
    block = pl.BlockSpec((tall, features), lambda i: (i, 0))
    return pl.pallas_call(
        functools.partial(update_kernel, 512 if features % 512 == 0 else 128),
        out_shape=jax.ShapeDtypeStruct((units, features), jnp.bfloat16),
        grid=(units // tall,),
        in_specs=[
            pl.BlockSpec((groups, tall, rows), lambda i: (0, i, 0)),
            pl.BlockSpec(cot_whole.shape, lambda i: (0, 0)),
            block,
            block,
        ],
        out_specs=block,
        compiler_params=pltpu.CompilerParams(vmem_limit_bytes=56 * 2**20),
        cost_estimate=pl.CostEstimate(
            flops=2 * groups * rows * units * features,
            bytes_accessed=6 * units * features,
            transcendentals=2 * units * features,
        ),
        name="update",
    )(hid_all, cot_whole, first_moment, second_moment)


def shards(pre_act, cotangent, down_weight, first_moment, second_moment):
    cot_all, hid_all, mine, away = exchange(pre_act, cotangent, down_weight)
    arrived = lax.ppermute(away, "dp", [(0, 2), (1, 3), (2, 0), (3, 1)])
    cot_whole = cot_all.reshape(-1, cot_all.shape[-1])
    step_update = update(hid_all, cot_whole, first_moment, second_moment)
    hidden_grad = mine.astype(jnp.float32) + arrived.astype(jnp.float32)
    input_grad = (hidden_grad * gelu_slopes(pre_act.astype(jnp.float32))).astype(jnp.bfloat16)
    return (input_grad, step_update)


def shards_any(pre_act, cotangent, down_weight, first_moment, second_moment):
    cot_whole = lax.all_gather(cotangent, "mp", axis=0, tiled=True)
    hidden = gelu_output(pre_act.astype(jnp.float32)).astype(jnp.bfloat16)
    hid_all = lax.all_gather(hidden.T, "dp", axis=0)
    partial_sum = lax.dot_general(
        cot_whole, down_weight, (((1,), (1,)), ((), ())), preferred_element_type=jnp.float32
    ).astype(jnp.bfloat16)
    hidden_grad = lax.psum_scatter(
        partial_sum, "dp", scatter_dimension=0, tiled=True
    ).astype(jnp.float32)
    step_update = update(hid_all, cot_whole, first_moment, second_moment)
    input_grad = (hidden_grad * gelu_slopes(pre_act.astype(jnp.float32))).astype(jnp.bfloat16)
    return (input_grad, step_update)


def solution(mesh):
    placed = (P("dp", "mp"), P("mp", "dp"), P("mp", "dp"), P("mp", "dp"), P("mp", "dp"))
    small = mesh.shape["mp"] == 8 and mesh.shape["dp"] == 4
    return jax.shard_map(
        shards if small else shards_any,
        mesh=mesh,
        in_specs=placed,
        out_specs=(P("dp", "mp"), P("mp", "dp")),
        check_vma=False,
    )
```

```python
import functools

import jax
import jax.numpy as jnp
from jax import lax
from jax.experimental import pallas as pl
from jax.experimental.pallas import tpu as pltpu
from jax.sharding import PartitionSpec as P

STEP = 20

MESH = pl.DeviceIdType.MESH

gelu_scale = 0.7978845608028654
gelu_cubic = 0.044715
beta_one = 0.9
beta_two = 0.95
epsilon = 1e-08


def gelu_output(values):
    tangent = jnp.tanh(gelu_scale * (values + gelu_cubic * values * values * values))
    return 0.5 * values * (1.0 + tangent)


def gelu_slopes(values):
    tangent = jnp.tanh(gelu_scale * (values + gelu_cubic * values * values * values))
    return 0.5 * (1.0 + tangent) + 0.5 * values * (1.0 - tangent * tangent) * gelu_scale * (
        1.0 + 3.0 * gelu_cubic * values * values
    )


def adam_step(gradient, first, second):
    root = ((1.0 - beta_two) / (1.0 - beta_two**STEP)) ** 0.5
    gain = (1.0 - beta_one) / (1.0 - beta_one**STEP) / root
    kind = gradient.dtype
    moment_one = kind.type(beta_one / (1.0 - beta_one)) * first + gradient
    moment_two = kind.type(beta_two / (1.0 - beta_two)) * second + gradient * gradient
    scaled = moment_two * lax.rsqrt(moment_two) + kind.type(epsilon / root)
    return kind.type(gain) * moment_one * pl.reciprocal(scaled, approx=True)


def exchange_kernel(
    chunks, pieces, block,
    pre_ref, cot_ref, weight_ref,
    cot_all, hid_all, mine_ref, away_ref,
    weight, hidden, total, part, other,
    weight_sem, own_sem, ring_send, ring_recv, hid_send, hid_recv, fwd_send, fwd_recv,
    pair_send, pair_recv,
):
    mp, dp = lax.axis_index("mp"), lax.axis_index("dp")
    tokens, features = cot_ref.shape
    units = weight_ref.shape[0]
    wide = features // chunks
    tall = units // pieces
    rows = pre_ref.shape[0]

    x, z = mp % 2, mp // 2
    place = z + x * (7 - 2 * z)

    def index_of(position):
        p = (position + 16) % 8
        side = p // 4
        return 2 * (p + side * (7 - 2 * p)) + side

    ring = (index_of(place + 1), index_of(place - 1))
    core, y = dp % 2, dp // 2
    sibling = 2 * y + (1 - core)
    across = 2 * (1 - y) + core

    def columns(k):
        return pl.ds(k * wide, wide)

    loads = []
    for k in range(chunks):
        load = pltpu.make_async_copy(
            weight_ref.at[:, columns(k)], weight.at[:, columns(k)], weight_sem.at[k]
        )
        load.start()
        loads.append(load)

    barrier = pltpu.get_barrier_semaphore()
    for position in ring:
        pl.semaphore_signal(barrier, inc=1, device_id={"mp": position}, device_id_type=MESH)
    for position in (sibling, across):
        pl.semaphore_signal(barrier, inc=1, device_id={"dp": position}, device_id_type=MESH)
    cot_all[mp] = cot_ref[...]
    pl.semaphore_wait(barrier, 4)

    def hops(k, way):
        return 4 if k % 2 == way else 3

    def ring_copy(k, hop, way):
        origin = index_of(place - hop if way == 0 else place + hop)
        return pltpu.make_async_remote_copy(
            src_ref=cot_all.at[origin, :, columns(k)],
            dst_ref=cot_all.at[origin, :, columns(k)],
            send_sem=ring_send.at[k, hop, way],
            recv_sem=ring_recv.at[k, hop, way],
            device_id={"mp": ring[way]},
            device_id_type=MESH,
        )

    def ring_wait(k, hop, way):
        origin = index_of(place - hop - 1 if way == 0 else place + hop + 1)
        pltpu.make_async_remote_copy(
            src_ref=cot_all.at[origin, :, columns(k)],
            dst_ref=cot_all.at[origin, :, columns(k)],
            send_sem=ring_send.at[k, hop, way],
            recv_sem=ring_recv.at[k, hop, way],
            device_id={"mp": ring[way]},
            device_id_type=MESH,
        ).wait_recv()

    def hid_rows(j):
        return pl.ds(j * tall, tall)

    def hid_copy(j, which):
        return pltpu.make_async_remote_copy(
            src_ref=hidden.at[hid_rows(j), :],
            dst_ref=hid_all.at[dp, hid_rows(j), :],
            send_sem=hid_send.at[j, which],
            recv_sem=hid_recv.at[j, which],
            device_id={"dp": (across, sibling)[which]},
            device_id_type=MESH,
        )

    def hid_wait(j, which):
        origin = (across, sibling)[which]
        pltpu.make_async_remote_copy(
            src_ref=hidden.at[hid_rows(j), :],
            dst_ref=hid_all.at[origin, hid_rows(j), :],
            send_sem=hid_send.at[j, which],
            recv_sem=hid_recv.at[j, which],
            device_id={"dp": origin},
            device_id_type=MESH,
        ).wait_recv()

    def forward_copy(j, origin):
        return pltpu.make_async_remote_copy(
            src_ref=hid_all.at[origin, hid_rows(j), :],
            dst_ref=hid_all.at[origin, hid_rows(j), :],
            send_sem=fwd_send.at[j],
            recv_sem=fwd_recv.at[j],
            device_id={"dp": sibling},
            device_id_type=MESH,
        )

    sent = []
    kept = []
    def ring_begin(k):
        for way in (0, 1):
            copy = ring_copy(k, 0, way)
            copy.start()
            sent.append(copy)

    def hid_begin(j):
        values = pre_ref[:, j * tall : (j + 1) * tall].astype(jnp.float32)
        hidden[hid_rows(j), :] = gelu_output(values).T.astype(jnp.bfloat16)
        for which in (0, 1):
            copy = hid_copy(j, which)
            copy.start()
            sent.append(copy)
        copy = pltpu.make_async_copy(
            hidden.at[hid_rows(j), :], hid_all.at[dp, hid_rows(j), :], own_sem.at[j]
        )
        copy.start()
        kept.append(copy)

    for ahead in (0, 1):
        ring_begin(ahead)
        hid_begin(ahead)

    def multiply(k, first, last):
        loads[k].wait()
        cot = cot_all[:, :, k * wide : (k + 1) * wide].reshape(8 * tokens, wide)

        span = block if last else 2 * block

        def one(i, carry):
            at = pl.ds(pl.multiple_of(i * span, span), span)
            product = lax.dot_general(
                cot,
                weight[at, columns(k)],
                (((1,), (1,)), ((), ())),
                preferred_element_type=jnp.float32,
            )
            if not first:
                product = product + total[:, at]
            if not last:
                total[:, at] = product
                return carry
            part[:, :, at] = product.astype(jnp.bfloat16).reshape(4, rows, block)
            for side in (0, 1):
                pair_copy(i, side).start()
            return carry

        lax.fori_loop(0, units // span, one, 0)

    def pair_copy(i, side):
        at = pl.ds(pl.multiple_of(i * block, block), block)
        return pltpu.make_async_remote_copy(
            src_ref=part.at[2 * side + 1 - core, :, at],
            dst_ref=other.at[side, :, at],
            send_sem=pair_send.at[i, side],
            recv_sem=pair_recv.at[i, side],
            device_id={"dp": sibling},
            device_id_type=MESH,
        )

    for step in range(chunks + 3):
        done = None
        for k in range(chunks):
            hop = step - k
            if hop < 0 or hop > 3:
                continue
            for way in (0, 1):
                if hop < hops(k, way):
                    ring_wait(k, hop, way)
                    if hop + 1 < hops(k, way):
                        copy = ring_copy(k, hop + 1, way)
                        copy.start()
                        sent.append(copy)
            if hop == 3:
                done = k
        if step + 2 < chunks:
            ring_begin(step + 2)
        if step + 2 < pieces:
            hid_begin(step + 2)
        if 0 <= step - 2 < pieces:
            hid_wait(step - 2, 0)
            copy = forward_copy(step - 2, across)
            copy.start()
            sent.append(copy)
        if done is not None:
            multiply(done, done == 0, done == chunks - 1)

    def combine(i, carry):
        at = pl.ds(pl.multiple_of(i * block, block), block)
        for side in (0, 1):
            pair_copy(i, side).wait()
        mine = part[2 * y + core, :, at].astype(jnp.float32) + other[y, :, at].astype(jnp.float32)
        away = part[2 * (1 - y) + core, :, at].astype(jnp.float32) + other[1 - y, :, at].astype(
            jnp.float32
        )
        mine_ref[:, at] = mine.astype(jnp.bfloat16)
        away_ref[:, at] = away.astype(jnp.bfloat16)
        return carry

    lax.fori_loop(0, units // block, combine, 0)

    for j in range(pieces):
        hid_wait(j, 1)
        forward_copy(j, 2 * (1 - y) + (1 - core)).wait_recv()
    for copy in sent:
        copy.wait_send()
    for copy in kept:
        copy.wait()


def exchange(pre_act, cotangent, weight):
    rows, units = pre_act.shape
    tokens, features = cotangent.shape
    chunks, pieces, block = 5, 6, 768
    vmem = pl.BlockSpec(memory_space=pltpu.VMEM)
    hbm = pl.BlockSpec(memory_space=pl.ANY)
    bf16 = jnp.bfloat16
    dma = pltpu.SemaphoreType.DMA
    return pl.pallas_call(
        functools.partial(exchange_kernel, chunks, pieces, block),
        out_shape=(
            jax.ShapeDtypeStruct((8, tokens, features), bf16),
            jax.ShapeDtypeStruct((4, units, rows), bf16),
            jax.ShapeDtypeStruct((rows, units), bf16),
            jax.ShapeDtypeStruct((rows, units), bf16),
        ),
        in_specs=[vmem, vmem, hbm],
        out_specs=(vmem, hbm, vmem, vmem),
        scratch_shapes=[
            pltpu.VMEM((units, features), bf16),
            pltpu.VMEM((units, rows), bf16),
            pltpu.VMEM((8 * tokens, units), jnp.float32),
            pltpu.VMEM((4, rows, units), bf16),
            pltpu.VMEM((2, rows, units), bf16),
            dma((chunks,)),
            dma((pieces,)),
            dma((chunks, 4, 2)),
            dma((chunks, 4, 2)),
            dma((pieces, 2)),
            dma((pieces, 2)),
            dma((pieces,)),
            dma((pieces,)),
            dma((units // block, 2)),
            dma((units // block, 2)),
        ],
        compiler_params=pltpu.CompilerParams(
            collective_id=0, has_side_effects=True, vmem_limit_bytes=60 * 2**20
        ),
        name="exchange",
    )(pre_act, cotangent, weight)


def update_kernel(tile, hid_ref, cot_ref, first_ref, second_ref, out_ref):
    hidden = jnp.concatenate([hid_ref[i] for i in range(hid_ref.shape[0])], axis=1)
    spans = [slice(at, at + tile) for at in range(0, out_ref.shape[1], tile)]

    def product(span):
        return jnp.dot(hidden, cot_ref[:, span], preferred_element_type=jnp.float32).astype(
            jnp.bfloat16
        )

    coming = product(spans[0])
    for i, span in enumerate(spans):
        gradient = coming
        if i + 1 < len(spans):
            coming = product(spans[i + 1])
        out_ref[:, span] = adam_step(gradient, first_ref[:, span], second_ref[:, span])


def update(hid_all, cot_whole, first_moment, second_moment):
    units, features = first_moment.shape
    groups, _, rows = hid_all.shape
    tall = 384
    block = pl.BlockSpec((tall, features), lambda i: (i, 0))
    return pl.pallas_call(
        functools.partial(update_kernel, 512 if features % 512 == 0 else 128),
        out_shape=jax.ShapeDtypeStruct((units, features), jnp.bfloat16),
        grid=(units // tall,),
        in_specs=[
            pl.BlockSpec((groups, tall, rows), lambda i: (0, i, 0)),
            pl.BlockSpec(cot_whole.shape, lambda i: (0, 0)),
            block,
            block,
        ],
        out_specs=block,
        compiler_params=pltpu.CompilerParams(vmem_limit_bytes=56 * 2**20),
        cost_estimate=pl.CostEstimate(
            flops=2 * groups * rows * units * features,
            bytes_accessed=6 * units * features,
            transcendentals=2 * units * features,
        ),
        name="update",
    )(hid_all, cot_whole, first_moment, second_moment)


def shards(pre_act, cotangent, down_weight, first_moment, second_moment):
    cot_all, hid_all, mine, away = exchange(pre_act, cotangent, down_weight)
    arrived = lax.ppermute(away, "dp", [(0, 2), (1, 3), (2, 0), (3, 1)])
    cot_whole = cot_all.reshape(-1, cot_all.shape[-1])
    step_update = update(hid_all, cot_whole, first_moment, second_moment)
    hidden_grad = mine.astype(jnp.float32) + arrived.astype(jnp.float32)
    input_grad = (hidden_grad * gelu_slopes(pre_act.astype(jnp.float32))).astype(jnp.bfloat16)
    return (input_grad, step_update)


def shards_any(pre_act, cotangent, down_weight, first_moment, second_moment):
    cot_whole = lax.all_gather(cotangent, "mp", axis=0, tiled=True)
    hidden = gelu_output(pre_act.astype(jnp.float32)).astype(jnp.bfloat16)
    hid_all = lax.all_gather(hidden.T, "dp", axis=0)
    partial_sum = lax.dot_general(
        cot_whole, down_weight, (((1,), (1,)), ((), ())), preferred_element_type=jnp.float32
    ).astype(jnp.bfloat16)
    hidden_grad = lax.psum_scatter(
        partial_sum, "dp", scatter_dimension=0, tiled=True
    ).astype(jnp.float32)
    step_update = update(hid_all, cot_whole, first_moment, second_moment)
    input_grad = (hidden_grad * gelu_slopes(pre_act.astype(jnp.float32))).astype(jnp.bfloat16)
    return (input_grad, step_update)


def solution(mesh):
    placed = (P("dp", "mp"), P("mp", "dp"), P("mp", "dp"), P("mp", "dp"), P("mp", "dp"))
    small = mesh.shape["mp"] == 8 and mesh.shape["dp"] == 4
    return jax.shard_map(
        shards if small else shards_any,
        mesh=mesh,
        in_specs=placed,
        out_specs=(P("dp", "mp"), P("mp", "dp")),
        check_vma=False,
    )
```

```python
import functools

import jax
import jax.numpy as jnp
from jax import lax
from jax.experimental import pallas as pl
from jax.experimental.pallas import tpu as pltpu
from jax.sharding import PartitionSpec as P

STEP = 20

MESH = pl.DeviceIdType.MESH

gelu_scale = 0.7978845608028654
gelu_cubic = 0.044715
beta_one = 0.9
beta_two = 0.95
epsilon = 1e-08


def gelu_output(values):
    tangent = jnp.tanh(gelu_scale * (values + gelu_cubic * values * values * values))
    return 0.5 * values * (1.0 + tangent)


def gelu_slopes(values):
    tangent = jnp.tanh(gelu_scale * (values + gelu_cubic * values * values * values))
    return 0.5 * (1.0 + tangent) + 0.5 * values * (1.0 - tangent * tangent) * gelu_scale * (
        1.0 + 3.0 * gelu_cubic * values * values
    )


def adam_step(gradient, first, second):
    root = ((1.0 - beta_two) / (1.0 - beta_two**STEP)) ** 0.5
    gain = (1.0 - beta_one) / (1.0 - beta_one**STEP) / root
    kind = gradient.dtype
    moment_one = kind.type(beta_one / (1.0 - beta_one)) * first + gradient
    moment_two = kind.type(beta_two / (1.0 - beta_two)) * second + gradient * gradient
    scaled = moment_two * lax.rsqrt(moment_two) + kind.type(epsilon / root)
    return kind.type(gain) * moment_one * pl.reciprocal(scaled, approx=True)


def exchange_kernel(
    chunks, pieces, block,
    pre_ref, cot_ref, weight_ref,
    cot_out, hid_all, mine_ref, away_ref,
    weight, hidden, total, part, other, turned, cot_all,
    weight_sem, own_sem, ring_send, ring_recv, hid_send, hid_recv, fwd_send, fwd_recv,
    pair_send, pair_recv, out_sem,
):
    mp, dp = lax.axis_index("mp"), lax.axis_index("dp")
    tokens, features = cot_ref.shape
    units = weight_ref.shape[0]
    wide = features // chunks
    tall = units // pieces
    rows = pre_ref.shape[0]

    x, z = mp % 2, mp // 2
    place = z + x * (7 - 2 * z)

    def index_of(position):
        p = (position + 16) % 8
        side = p // 4
        return 2 * (p + side * (7 - 2 * p)) + side

    ring = (index_of(place + 1), index_of(place - 1))
    core, y = dp % 2, dp // 2
    sibling = 2 * y + (1 - core)
    across = 2 * (1 - y) + core

    def columns(k):
        return pl.ds(k * wide, wide)

    loads = []
    for k in range(chunks):
        load = pltpu.make_async_copy(
            weight_ref.at[:, columns(k)], weight.at[:, columns(k)], weight_sem.at[k]
        )
        load.start()
        loads.append(load)

    barrier = pltpu.get_barrier_semaphore()
    for position in ring:
        pl.semaphore_signal(barrier, inc=1, device_id={"mp": position}, device_id_type=MESH)
    for position in (sibling, across):
        pl.semaphore_signal(barrier, inc=1, device_id={"dp": position}, device_id_type=MESH)
    cot_all[mp] = cot_ref[...]
    pl.semaphore_wait(barrier, 4)

    def hops(k, way):
        return 4 if k % 2 == way else 3

    def ring_copy(k, hop, way):
        origin = index_of(place - hop if way == 0 else place + hop)
        return pltpu.make_async_remote_copy(
            src_ref=cot_all.at[origin, :, columns(k)],
            dst_ref=cot_all.at[origin, :, columns(k)],
            send_sem=ring_send.at[k, hop, way],
            recv_sem=ring_recv.at[k, hop, way],
            device_id={"mp": ring[way]},
            device_id_type=MESH,
        )

    def ring_wait(k, hop, way):
        origin = index_of(place - hop - 1 if way == 0 else place + hop + 1)
        pltpu.make_async_remote_copy(
            src_ref=cot_all.at[origin, :, columns(k)],
            dst_ref=cot_all.at[origin, :, columns(k)],
            send_sem=ring_send.at[k, hop, way],
            recv_sem=ring_recv.at[k, hop, way],
            device_id={"mp": ring[way]},
            device_id_type=MESH,
        ).wait_recv()

    def hid_rows(j):
        return pl.ds(j * tall, tall)

    def hid_copy(j, which):
        return pltpu.make_async_remote_copy(
            src_ref=hidden.at[hid_rows(j), :],
            dst_ref=hid_all.at[dp, hid_rows(j), :],
            send_sem=hid_send.at[j, which],
            recv_sem=hid_recv.at[j, which],
            device_id={"dp": (across, sibling)[which]},
            device_id_type=MESH,
        )

    def hid_wait(j, which):
        origin = (across, sibling)[which]
        pltpu.make_async_remote_copy(
            src_ref=hidden.at[hid_rows(j), :],
            dst_ref=hid_all.at[origin, hid_rows(j), :],
            send_sem=hid_send.at[j, which],
            recv_sem=hid_recv.at[j, which],
            device_id={"dp": origin},
            device_id_type=MESH,
        ).wait_recv()

    def forward_copy(j, origin):
        return pltpu.make_async_remote_copy(
            src_ref=hid_all.at[origin, hid_rows(j), :],
            dst_ref=hid_all.at[origin, hid_rows(j), :],
            send_sem=fwd_send.at[j],
            recv_sem=fwd_recv.at[j],
            device_id={"dp": sibling},
            device_id_type=MESH,
        )

    sent = []
    kept = []
    def ring_begin(k):
        for way in (0, 1):
            copy = ring_copy(k, 0, way)
            copy.start()
            sent.append(copy)

    def hid_begin(j):
        values = pre_ref[:, j * tall : (j + 1) * tall].astype(jnp.float32)
        hidden[hid_rows(j), :] = gelu_output(values).T.astype(jnp.bfloat16)
        for which in (0, 1):
            copy = hid_copy(j, which)
            copy.start()
            sent.append(copy)
        copy = pltpu.make_async_copy(
            hidden.at[hid_rows(j), :], hid_all.at[dp, hid_rows(j), :], own_sem.at[j]
        )
        copy.start()
        kept.append(copy)

    for ahead in (0, 1):
        ring_begin(ahead)
        hid_begin(ahead)

    def multiply(k, first, last):
        copy = pltpu.make_async_copy(
            cot_all.at[:, :, columns(k)], cot_out.at[:, :, columns(k)], out_sem.at[k]
        )
        copy.start()
        kept.append(copy)
        loads[k].wait()
        turned[...] = cot_all[:, :, k * wide : (k + 1) * wide].reshape(8 * tokens, wide).T

        span = block if last else 2 * block

        def one(i, carry):
            at = pl.ds(pl.multiple_of(i * span, span), span)
            product = jnp.dot(
                weight[at, columns(k)], turned[...], preferred_element_type=jnp.float32
            )
            if not first:
                product = product + total[at, :]
            if not last:
                total[at, :] = product
                return carry
            rounded = product.astype(jnp.bfloat16)
            for owner in range(4):
                part[owner, at, :] = rounded[:, owner * rows : (owner + 1) * rows]
            for side in (0, 1):
                pair_copy(i, side).start()
            return carry

        lax.fori_loop(0, units // span, one, 0)

    def pair_copy(i, side):
        at = pl.ds(pl.multiple_of(i * block, block), block)
        return pltpu.make_async_remote_copy(
            src_ref=part.at[2 * side + 1 - core, at, :],
            dst_ref=other.at[side, at, :],
            send_sem=pair_send.at[i, side],
            recv_sem=pair_recv.at[i, side],
            device_id={"dp": sibling},
            device_id_type=MESH,
        )

    for step in range(chunks + 3):
        done = None
        for k in range(chunks):
            hop = step - k
            if hop < 0 or hop > 3:
                continue
            for way in (0, 1):
                if hop < hops(k, way):
                    ring_wait(k, hop, way)
                    if hop + 1 < hops(k, way):
                        copy = ring_copy(k, hop + 1, way)
                        copy.start()
                        sent.append(copy)
            if hop == 3:
                done = k
        if step + 2 < chunks:
            ring_begin(step + 2)
        if step + 2 < pieces:
            hid_begin(step + 2)
        if 0 <= step - 2 < pieces:
            hid_wait(step - 2, 0)
            copy = forward_copy(step - 2, across)
            copy.start()
            sent.append(copy)
        if done is not None:
            multiply(done, done == 0, done == chunks - 1)

    def combine(i, carry):
        at = pl.ds(pl.multiple_of(i * block, block), block)
        for side in (0, 1):
            pair_copy(i, side).wait()
        for owner, out_ref in ((y, mine_ref), (1 - y, away_ref)):
            summed = part[2 * owner + core, at, :].astype(jnp.float32) + other[
                owner, at, :
            ].astype(jnp.float32)
            out_ref[:, at] = summed.T.astype(jnp.bfloat16)
        return carry

    lax.fori_loop(0, units // block, combine, 0)

    for j in range(pieces):
        hid_wait(j, 1)
        forward_copy(j, 2 * (1 - y) + (1 - core)).wait_recv()
    for copy in sent:
        copy.wait_send()
    for copy in kept:
        copy.wait()


def exchange(pre_act, cotangent, weight):
    rows, units = pre_act.shape
    tokens, features = cotangent.shape
    chunks, pieces, block = 5, 6, 768
    vmem = pl.BlockSpec(memory_space=pltpu.VMEM)
    hbm = pl.BlockSpec(memory_space=pl.ANY)
    bf16 = jnp.bfloat16
    dma = pltpu.SemaphoreType.DMA
    return pl.pallas_call(
        functools.partial(exchange_kernel, chunks, pieces, block),
        out_shape=(
            jax.ShapeDtypeStruct((8, tokens, features), bf16),
            jax.ShapeDtypeStruct((4, units, rows), bf16),
            jax.ShapeDtypeStruct((rows, units), bf16),
            jax.ShapeDtypeStruct((rows, units), bf16),
        ),
        in_specs=[vmem, vmem, hbm],
        out_specs=(hbm, hbm, vmem, vmem),
        scratch_shapes=[
            pltpu.VMEM((units, features), bf16),
            pltpu.VMEM((units, rows), bf16),
            pltpu.VMEM((units, 8 * tokens), jnp.float32),
            pltpu.VMEM((4, units, rows), bf16),
            pltpu.VMEM((2, units, rows), bf16),
            pltpu.VMEM((features // chunks, 8 * tokens), bf16),
            pltpu.VMEM((8, tokens, features), bf16),
            dma((chunks,)),
            dma((pieces,)),
            dma((chunks, 4, 2)),
            dma((chunks, 4, 2)),
            dma((pieces, 2)),
            dma((pieces, 2)),
            dma((pieces,)),
            dma((pieces,)),
            dma((units // block, 2)),
            dma((units // block, 2)),
            dma((chunks,)),
        ],
        compiler_params=pltpu.CompilerParams(
            collective_id=0, has_side_effects=True, vmem_limit_bytes=60 * 2**20
        ),
        name="exchange",
    )(pre_act, cotangent, weight)


def update_kernel(tile, hid_ref, cot_ref, first_ref, second_ref, out_ref):
    hidden = jnp.concatenate([hid_ref[i] for i in range(hid_ref.shape[0])], axis=1)
    spans = [slice(at, at + tile) for at in range(0, out_ref.shape[1], tile)]

    def product(span):
        return jnp.dot(hidden, cot_ref[:, span], preferred_element_type=jnp.float32).astype(
            jnp.bfloat16
        )

    coming = product(spans[0])
    for i, span in enumerate(spans):
        gradient = coming
        if i + 1 < len(spans):
            coming = product(spans[i + 1])
        out_ref[:, span] = adam_step(gradient, first_ref[:, span], second_ref[:, span])


def update(hid_all, cot_whole, first_moment, second_moment):
    units, features = first_moment.shape
    groups, _, rows = hid_all.shape
    tall = 512 if units % 512 == 0 else 384
    block = pl.BlockSpec((tall, features), lambda i: (i, 0))
    return pl.pallas_call(
        functools.partial(update_kernel, 512 if features % 512 == 0 else 128),
        out_shape=jax.ShapeDtypeStruct((units, features), jnp.bfloat16),
        grid=(units // tall,),
        in_specs=[
            pl.BlockSpec((groups, tall, rows), lambda i: (0, i, 0)),
            pl.BlockSpec(cot_whole.shape, lambda i: (0, 0)),
            block,
            block,
        ],
        out_specs=block,
        compiler_params=pltpu.CompilerParams(vmem_limit_bytes=56 * 2**20),
        cost_estimate=pl.CostEstimate(
            flops=2 * groups * rows * units * features,
            bytes_accessed=6 * units * features,
            transcendentals=2 * units * features,
        ),
        name="update",
    )(hid_all, cot_whole, first_moment, second_moment)


def shards(pre_act, cotangent, down_weight, first_moment, second_moment):
    cot_all, hid_all, mine, away = exchange(pre_act, cotangent, down_weight)
    arrived = lax.ppermute(away, "dp", [(0, 2), (1, 3), (2, 0), (3, 1)])
    cot_whole = cot_all.reshape(-1, cot_all.shape[-1])
    step_update = update(hid_all, cot_whole, first_moment, second_moment)
    hidden_grad = mine.astype(jnp.float32) + arrived.astype(jnp.float32)
    input_grad = (hidden_grad * gelu_slopes(pre_act.astype(jnp.float32))).astype(jnp.bfloat16)
    return (input_grad, step_update)


def shards_any(pre_act, cotangent, down_weight, first_moment, second_moment):
    cot_whole = lax.all_gather(cotangent, "mp", axis=0, tiled=True)
    hidden = gelu_output(pre_act.astype(jnp.float32)).astype(jnp.bfloat16)
    hid_all = lax.all_gather(hidden.T, "dp", axis=0)
    partial_sum = lax.dot_general(
        cot_whole, down_weight, (((1,), (1,)), ((), ())), preferred_element_type=jnp.float32
    ).astype(jnp.bfloat16)
    hidden_grad = lax.psum_scatter(
        partial_sum, "dp", scatter_dimension=0, tiled=True
    ).astype(jnp.float32)
    step_update = update(hid_all, cot_whole, first_moment, second_moment)
    input_grad = (hidden_grad * gelu_slopes(pre_act.astype(jnp.float32))).astype(jnp.bfloat16)
    return (input_grad, step_update)


def solution(mesh):
    placed = (P("dp", "mp"), P("mp", "dp"), P("mp", "dp"), P("mp", "dp"), P("mp", "dp"))
    small = mesh.shape["mp"] == 8 and mesh.shape["dp"] == 4
    return jax.shard_map(
        shards if small else shards_any,
        mesh=mesh,
        in_specs=placed,
        out_specs=(P("dp", "mp"), P("mp", "dp")),
        check_vma=False,
    )
```
